128 devices in a mesh: row: 8 (over y, core), col: 16 (over x, z).
Axes of the slice: x: 4, y: 4, z: 4, core: 2. Of those that a mesh axis runs over, the one named last changes fastest.
Arguments:
- probes: float32 [131072, 256], P(('row', 'col')), may hold values from -6 to 6
- near_blocks: bfloat16 [128, 8, 1024, 1024], P(('row', 'col')), may hold values from -0.09375 to 0.09375
- near_leaves: int32 [128, 8], P(('row', 'col')), may hold values from 0 to 15, as said below
- near_count: int32 [128], P(('row', 'col')), may hold values from 1 to 8, as said below
- leaf_rank: int32 [128], P(('row', 'col')), may hold values from 128 to 256
- leaf_basis: float32 [131072, 256], P(('row', 'col')), may hold values from -0.1875 to 0.1875
- leaf_transfer: float32 [128, 256, 512], P(('row', 'col')), may hold values from -0.09375 to 0.09375
- leaf_links: int32 [128, 4], P(('row', 'col')), may hold values from 0 to 15, as said below
- leaf_link_blocks: float32 [128, 4, 256, 256], P(('row', 'col')), may hold values from -0.1875 to 0.1875
- parent_links: int32 [8, 2], P('row'), may hold values from 0 to 7, as said below
- parent_link_blocks: float32 [8, 2, 512, 512], P('row'), may hold values from -0.1875 to 0.1875
Outputs:
- term_one: float32 [131072, 256], P(('row', 'col'))
- term_two: float32 [131072, 256], P(('row', 'col'))
The draws below stay inside these ranges and needn't reach their ends.
Inputs may be any that keep to these rules, and one draw needn't show every extreme that they name: `near_leaves`: slot 0 of every leaf is the leaf's own position; slots 1 to near_count - 1 are distinct other positions of the same group; later slots repeat the leaf's own position. `near_count`: some leaf has 8 live slots in every draw. `leaf_links`: each leaf's 4 coupled positions are distinct and differ from its own. `parent_links`: each parent's 2 coupled parents are distinct and differ from itself.
All inputs are finite; a program needn't handle non-finite values.
Results may differ from the reference program's by a relative error of at most 0.0034.
Values may be sent and summed in bfloat16 or wider, within the bound.
A program may use at most 128 MiB of HBM per device.

```python
import jax
import jax.numpy as jnp
from jax import lax

LEAF = 1024
RANK_LEAF = 256
RANK_PARENT = 512
PROBES = 256
NEAR_MAX = 8
LC_MAX = 4
PC_MAX = 2
GROUPS = 8
GROUP_LEAVES = 16
LEAVES = 128
ORDER = 131072


def near_tables(key):
    base = jax.random.fold_in(key, 11)
    key_order = jax.random.fold_in(base, 1)
    key_count = jax.random.fold_in(base, 2)
    leaves = jnp.arange(LEAVES, dtype=jnp.int32)
    column = leaves % GROUP_LEAVES
    steps_away = jnp.arange(1, GROUP_LEAVES, dtype=jnp.int32)
    candidate = (column[:, None] + steps_away[None, :]) % GROUP_LEAVES
    scores = jax.random.randint(key_order, (LEAVES, GROUP_LEAVES - 1), 0, 1 << 20) * GROUP_LEAVES + steps_away[None, :]
    halfway = (steps_away == GROUP_LEAVES // 2)[None, :] & (leaves == 4)[:, None]
    scores = jnp.where(halfway, jnp.int32(-1), scores)
    ranking = jnp.argsort(scores, axis=1)
    picked = jnp.take_along_axis(candidate, ranking, axis=1)[:, :NEAR_MAX - 1]
    counts = jax.random.randint(key_count, (LEAVES,), 1, NEAR_MAX + 1)
    counts = counts.at[4].set(NEAR_MAX)
    listing = jnp.concatenate([column[:, None], picked], axis=1)
    slot_ids = jnp.arange(NEAR_MAX, dtype=jnp.int32)
    listing = jnp.where(slot_ids[None, :] < counts[:, None], listing, column[:, None])
    return (listing.astype(jnp.int32), counts.astype(jnp.int32))


def draw_near_leaves(key, part):
    return near_tables(key)[0]


def draw_near_count(key, part):
    return near_tables(key)[1]


def distinct_others(key, total, width, salt):
    base = jax.random.fold_in(key, salt)
    leaf_keys = jax.random.split(base, total)
    steps_away = jax.vmap(lambda leaf_key: jax.random.permutation(leaf_key, width - 1))(leaf_keys)
    return steps_away + 1


def draw_leaf_links(key, part):
    steps_away = distinct_others(key, LEAVES, GROUP_LEAVES, 23)[:, :LC_MAX]
    column = jnp.arange(LEAVES, dtype=jnp.int32) % GROUP_LEAVES
    return ((column[:, None] + steps_away) % GROUP_LEAVES).astype(jnp.int32)


def draw_parent_links(key, part):
    steps_away = distinct_others(key, GROUPS, GROUPS, 37)[:, :PC_MAX]
    owners = jnp.arange(GROUPS, dtype=jnp.int32)
    return ((owners[:, None] + steps_away) % GROUPS).astype(jnp.int32)


def with_ends(values, rng, smallest, largest):
    longest = values.shape.index(max(values.shape))
    spots = []
    for shift in (0, 1):
        where = [jax.random.randint(jax.random.fold_in(rng, axis), (), 0, length) for axis, length in enumerate(values.shape)]
        where[longest] = (where[longest] + shift) % values.shape[longest]
        spots.append(tuple(where))
    return values.at[spots[0]].set(smallest).at[spots[1]].set(largest)


def block_scale(rng, extent, shards, least, high):
    def one(position, blocks):
        heights = jax.random.uniform(jax.random.fold_in(jax.random.fold_in(rng, 6), position), (blocks,), jnp.float32, least / len(shards), high / len(shards))
        return jnp.repeat(jnp.exp(heights), extent[position] // blocks).reshape((-1,) + (1,) * (len(extent) - position - 1))

    factor_of = one(*shards[0])
    for cut in shards[1:]:
        factor_of = factor_of * one(*cut)
    return factor_of


def scatter_about(rng, extent, scale, limit, cuts=(), kind=jnp.bfloat16):
    array = scale * jax.random.normal(rng, extent, jnp.float32)
    if cuts:
        array = array * block_scale(rng, extent, cuts, -0.22, 0.18)
    return jnp.clip(array, -limit, limit).astype(kind)


def setup_inputs(seed: int = 0) -> dict:
    key_list = jax.random.split(jax.random.key(seed), 12)
    return {
        "probes": scatter_about(key_list[0], (ORDER, PROBES), 1.0, 6.0, ((0, 128),), jnp.float32),
        "near_blocks": scatter_about(key_list[1], (LEAVES, NEAR_MAX, LEAF, LEAF), (4 * LEAF) ** -0.5, 0.09375, ((0, 128),)),
        "near_leaves": draw_near_leaves(jax.random.fold_in(key_list[11], 71), 0),
        "near_count": draw_near_count(jax.random.fold_in(key_list[11], 71), 0),
        "leaf_rank": with_ends(jax.random.randint(key_list[4], (LEAVES,), RANK_LEAF // 2, RANK_LEAF + 1), jax.random.fold_in(key_list[4], 1), RANK_LEAF // 2, RANK_LEAF).astype(jnp.int32),
        "leaf_basis": scatter_about(key_list[5], (ORDER, RANK_LEAF), LEAF ** -0.5, 0.1875, ((0, 128),), jnp.float32),
        "leaf_transfer": scatter_about(key_list[6], (LEAVES, RANK_LEAF, RANK_PARENT), (RANK_LEAF * GROUP_LEAVES) ** -0.5, 0.09375, ((0, 128),), jnp.float32),
        "leaf_links": draw_leaf_links(jax.random.fold_in(key_list[11], 71), 0),
        "leaf_link_blocks": scatter_about(key_list[8], (LEAVES, LC_MAX, RANK_LEAF, RANK_LEAF), (RANK_LEAF * LC_MAX) ** -0.5, 0.1875, ((0, 128),), jnp.float32),
        "parent_links": draw_parent_links(jax.random.fold_in(key_list[11], 71), 0),
        "parent_link_blocks": scatter_about(key_list[10], (GROUPS, PC_MAX, RANK_PARENT, RANK_PARENT), (RANK_PARENT * PC_MAX) ** -0.5, 0.1875, ((0, 8),), jnp.float32),
    }


def kernel_product(vector, near_blocks, near_leaves, near_count, leaf_rank, leaf_basis, leaf_transfer, leaf_links, leaf_link_blocks, parent_links, parent_link_blocks):
    highest = lax.Precision.HIGHEST
    owners = jnp.arange(LEAVES, dtype=jnp.int32) // GROUP_LEAVES
    packed = vector.astype(jnp.bfloat16).reshape(LEAVES, LEAF, PROBES)
    blocks_in = vector.reshape(LEAVES, LEAF, PROBES)
    basis = leaf_basis.reshape(LEAVES, LEAF, RANK_LEAF)
    rank_mask = (jnp.arange(RANK_LEAF, dtype=jnp.int32)[None, :] < leaf_rank[:, None]).astype(jnp.float32)[:, :, None]

    def near_leaf(leaf):
        sources = (owners[leaf] * GROUP_LEAVES + near_leaves[leaf]).astype(jnp.int32)

        def add_slot(slot, total):
            near_block = near_blocks[leaf, slot].astype(jnp.float32)
            source = packed[sources[slot]].astype(jnp.float32)
            return total + jnp.dot(near_block, source, precision=highest)

        return lax.fori_loop(0, near_count[leaf], add_slot, jnp.zeros((LEAF, PROBES), jnp.float32))

    near_sum = lax.map(near_leaf, jnp.arange(LEAVES, dtype=jnp.int32))
    skeleton = jnp.einsum('lir,lip->lrp', basis, blocks_in, precision=highest) * rank_mask
    linked = skeleton[(owners[:, None] * GROUP_LEAVES + leaf_links).astype(jnp.int32)]
    coupled = jnp.einsum('lkab,lkbp->lap', leaf_link_blocks, linked, precision=highest)
    upward = jnp.einsum('lrq,lrp->lqp', leaf_transfer, skeleton, precision=highest)
    parents = upward.reshape(GROUPS, GROUP_LEAVES, RANK_PARENT, PROBES).sum(axis=1)
    far_parent = jnp.einsum('gkab,gkbp->gap', parent_link_blocks, parents[parent_links], precision=highest)
    downward = jnp.einsum('lrq,lqp->lrp', leaf_transfer, far_parent[owners], precision=highest)
    combined = (coupled + downward) * rank_mask
    result = jnp.einsum('lir,lrp->lip', basis, combined, precision=highest) + near_sum
    return result.reshape(LEAVES * LEAF, PROBES)


def reference(probes, near_blocks, near_leaves, near_count, leaf_rank, leaf_basis, leaf_transfer, leaf_links, leaf_link_blocks, parent_links, parent_link_blocks):
    tables = (near_blocks, near_leaves, near_count, leaf_rank, leaf_basis, leaf_transfer, leaf_links, leaf_link_blocks, parent_links, parent_link_blocks)
    term_one = kernel_product(probes, *tables)
    term_two = 2.0 * kernel_product(term_one, *tables) - probes
    return term_one, term_two
```

```python
import functools

import jax
import jax.numpy as jnp
from jax import lax
from jax.experimental import pallas as pl
from jax.experimental.pallas import tpu as pltpu
from jax.sharding import PartitionSpec as P

BF = jnp.bfloat16
F32 = jnp.float32
SIDE = 4
PEERS = SIDE * SIDE
LEAF = 1024
HALF = LEAF // 2
RANK = 256
PARENT = 512
PROBES = 256
CHUNKS = 2
COLS = PROBES // CHUNKS
STAGES = 2 * CHUNKS
BLOCK = HALF + RANK // 2
PIECE = BLOCK // 2
SHARE = PROBES // CHUNKS // PEERS


def dot(a, b, ca=1, cb=0):
    return lax.dot_general(a, b, (((ca,), (cb,)), ((), ())), preferred_element_type=F32)


def split(value):
    high = value.astype(BF)
    return high, (value - high.astype(F32)).astype(BF)


def dot_split(ah, al, bh, bl):
    return dot(ah, bh) + (dot(al, bh) + dot(ah, bl))


def fold(value):
    return jnp.concatenate([value[:, : PARENT // 2], value[:, PARENT // 2 :]], axis=0)


def unfold(value):
    return jnp.concatenate([value[:SHARE], value[SHARE:]], axis=1)


def kernel(
    rows,
    near_leaves, near_count, leaf_rank, leaf_links, parent_links,
    probes, near, basis, transfer, link_blocks, parent_blocks,
    out_one, out_two,
    g, near_buf, v_buf, acc, coup, t_buf,
    basis_f, transfer_f, link_f, parent_f,
    u_hi, u_lo, ut_hi, ut_lo, e_bf, l_bf, b_bf,
    up_send, up_recv, par, far_recv,
    near_slot, near_has, link_slot, link_has,
    load_sem, out_sem, g_send, g_recv, up_ss, up_rs, row_ss, row_rs, far_ss, far_rs,
):
    row = lax.axis_index("row")
    me = lax.axis_index("col")
    x, z = me // SIDE, me % SIDE

    loads = [
        pltpu.make_async_copy(src, dst, load_sem.at[i])
        for i, (src, dst) in enumerate(
            (
                (probes, v_buf),
                (basis, basis_f),
                (transfer.at[0], transfer_f),
                (link_blocks.at[0], link_f),
                (parent_blocks.at[0], parent_f),
                (near.at[0], near_buf),
            )
        )
    ]
    for load in loads:
        load.start()

    barrier = pltpu.get_barrier_semaphore()
    for d in range(1, PEERS):
        pl.semaphore_signal(barrier, inc=1, device_id={"col": (me + d) % PEERS})
    for d in range(1, rows):
        pl.semaphore_signal(barrier, inc=1, device_id={"row": (row + d) % rows})

    count = near_count[0]
    for a in range(SIDE):
        for b in range(SIDE):
            source = ((x + SIDE - a) % SIDE) * SIDE + (z + SIDE - b) % SIDE
            slot, has = jnp.int32(0), jnp.int32(0)
            for k in range(8):
                hit = jnp.logical_and(near_leaves[0, k] == source, k < count)
                slot, has = jnp.where(hit, k, slot), jnp.where(hit, 1, has)
            near_slot[a * SIDE + b] = slot
            near_has[a * SIDE + b] = has
            slot, has = jnp.int32(0), jnp.int32(0)
            for k in range(4):
                hit = leaf_links[0, k] == source
                slot, has = jnp.where(hit, k, slot), jnp.where(hit, 1, has)
            link_slot[a * SIDE + b] = slot
            link_has[a * SIDE + b] = has

    rank = leaf_rank[0]
    mask = lax.broadcasted_iota(jnp.int32, (RANK, COLS), 0) < rank

    def masked(value):
        return jnp.where(mask, value, jnp.zeros_like(value))

    def slot_of(half, p, q):
        return p * SIDE + q if half == 0 else q * SIDE + p

    def at_step(half, first, step):
        along_x = first == (half == 0)
        if along_x:
            return {"col": ((x + step + SIDE) % SIDE) * SIDE + z}
        return {"col": x * SIDE + (z + step + SIDE) % SIDE}

    def send(s, half, source, target, first, step, piece=None):
        src, dst = g.at[s, half, source], g.at[s, half, target]
        if piece is not None:
            part = pl.ds(piece * PIECE, PIECE)
            src, dst = src.at[part], dst.at[part]
        pltpu.make_async_remote_copy(
            src_ref=src,
            dst_ref=dst,
            send_sem=g_send.at[s, half],
            recv_sem=g_recv.at[s, half, target],
            device_id=at_step(half, first, step),
        ).start()

    def along_first(s, half, step, piece=None):
        source = slot_of(half, 0, 0) if piece is None else slot_of(half, step % SIDE, 0)
        target = slot_of(half, (step if piece is None else 2) % SIDE, 0)
        send(s, half, source, target, True, step, piece)

    def along_second(s, half, p, step, piece=None):
        source = slot_of(half, p, 0 if piece is None else step % SIDE)
        target = slot_of(half, p, (step if piece is None else 2) % SIDE)
        send(s, half, source, target, False, step, piece)

    def send_own(s):
        for half in range(2):
            for step in (1, -1):
                along_first(s, half, step)
            for step in (1, -1):
                along_second(s, half, 0, step)

    def arrive(s, half, p, q):
        slot = slot_of(half, p, q)
        ref = g.at[s, half, slot]
        pltpu.make_async_copy(ref, ref, g_recv.at[s, half, slot]).wait()
        if q == 0:
            if p == 1:
                along_first(s, half, 1, 0)
            if p == 3:
                along_first(s, half, -1, 1)
            along_second(s, half, p, 1)
            along_second(s, half, p, -1)
        elif q == 1:
            along_second(s, half, p, 1, 0)
        elif q == 3:
            along_second(s, half, p, -1, 1)

    def product(s, half, slot):
        block = g[s, half, slot, :HALF]
        block = jnp.where(near_has[slot] > 0, block, jnp.zeros_like(block))
        acc[...] += dot(near_buf[near_slot[slot], :, half * HALF : (half + 1) * HALF], block)
        block = g[s, half, slot, HALF:]
        block = jnp.where(link_has[slot] > 0, block, jnp.zeros_like(block))
        width = RANK // 2
        coup[...] += dot(l_bf[link_slot[slot], :, half * width : (half + 1) * width], block)

    def make_message(s, v):
        high, low = split(v)
        skeleton = masked(dot_split(ut_hi[...], ut_lo[...], high, low))
        packed = skeleton.astype(BF)
        for half in range(2):
            g[s, half, 0, :HALF] = high[half * HALF : (half + 1) * HALF]
            g[s, half, 0, HALF:] = packed[half * RANK // 2 : (half + 1) * RANK // 2]
        return skeleton

    def to_peers(src_of, dst_of, ss, rs):
        for d in range(1, PEERS):
            peer = (me + d) % PEERS
            pltpu.make_async_remote_copy(
                src_ref=src_of(peer), dst_ref=dst_of(d), send_sem=ss, recv_sem=rs, device_id={"col": peer}
            ).start()

    def upward(s, skeleton):
        up = dot(skeleton.T.astype(BF), e_bf[...])
        for j in range(PEERS):
            up_send[s, j] = fold(up[j * SHARE : (j + 1) * SHARE]).astype(BF)
        up_recv[s, 0] = up_send[s, me]
        to_peers(
            lambda peer: up_send.at[s, peer], lambda d: up_recv.at[s, d], up_ss.at[s], up_rs.at[s]
        )

    def wait_all(ref, sem):
        pltpu.make_async_copy(ref, ref, sem).wait()

    def parents(s):
        wait_all(up_recv.at[s, pl.ds(1, PEERS - 1)], up_rs.at[s])
        total = up_recv[s, 0].astype(F32)
        for d in range(1, PEERS):
            total += up_recv[s, d].astype(F32)
        par[s, 0] = total.astype(BF)
        for d in range(1, rows):
            pltpu.make_async_remote_copy(
                src_ref=par.at[s, 0],
                dst_ref=par.at[s, d],
                send_sem=row_ss.at[s],
                recv_sem=row_rs.at[s],
                device_id={"row": (row + d) % rows},
            ).start()

    def far(s):
        wait_all(par.at[s, pl.ds(1, rows - 1)], row_rs.at[s])
        total = jnp.zeros((SHARE, PARENT), F32)
        for k in range(2):
            away = (row + rows - parent_links[0, k]) % rows
            source = jnp.zeros((2 * SHARE, PARENT // 2), F32)
            for d in range(1, rows):
                source = jnp.where(away == d, par[s, d].astype(F32), source)
            source = source.astype(BF)
            total += dot(source, b_bf[k, :, : PARENT // 2], 1, 1)[:SHARE]
            total += dot(source, b_bf[k, :, PARENT // 2 :], 1, 1)[SHARE:]
        far_recv[s, me] = fold(total).astype(BF)
        to_peers(
            lambda peer: far_recv.at[s, me], lambda d: far_recv.at[s, me], far_ss.at[s], far_rs.at[s]
        )

    def combined_result(s):
        wait_all(far_recv.at[s, pl.ds(0, PEERS - 1)], far_rs.at[s])
        far_parent = jnp.concatenate(
            [unfold(far_recv[s, j].astype(F32)) for j in range(PEERS)], axis=0
        ).astype(BF)
        high, low = split(masked(coup[...] + dot(e_bf[...], far_parent, 1, 1)))
        return dot_split(u_hi[...], u_lo[...], high, low) + acc[...]

    loads[0].wait()
    loads[1].wait()
    u = basis_f[...]
    u_hi[...], u_lo[...] = split(u)
    ut_hi[...], ut_lo[...] = split(u.T)
    pl.semaphore_wait(barrier, PEERS - 1 + rows - 1)
    first = make_message(0, v_buf[:, :COLS])
    send_own(0)
    loads[2].wait()
    e_bf[...] = transfer_f[...].astype(BF)
    upward(0, first)
    for c in range(1, CHUNKS):
        upward(c, make_message(c, v_buf[:, c * COLS : (c + 1) * COLS]))
    loads[3].wait()
    l_bf[...] = link_f[...].astype(BF)
    loads[4].wait()
    b_bf[...] = parent_f[...].astype(BF)
    loads[5].wait()

    events = [(1, 0), (3, 0), (0, 1), (0, 3), (2, 0)]
    events += [(p, q) for p in (1, 3, 2) for q in (1, 3)]
    events += [(0, 2), (1, 2), (3, 2), (2, 2)]
    events = [(half, p, q) for p, q in events for half in range(2)]

    @pl.loop(0, STAGES)
    def _(s):
        acc[...] = jnp.zeros_like(acc)
        coup[...] = jnp.zeros_like(coup)
        columns = pl.ds(pl.multiple_of((s % CHUNKS) * COLS, COLS), COLS)
        for half in range(2):
            product(s, half, 0)
        for i, (half, p, q) in enumerate(events):
            arrive(s, half, p, q)
            product(s, half, slot_of(half, p, q))
            if i == 5:
                pl.when(s == 0)(lambda: parents(0))
            if i == 9:
                pl.when(s == 0)(lambda: far(0))
            if i == 7:
                pl.when(s + 1 < STAGES)(lambda: parents(s + 1))
            if i == 15:
                pl.when(s + 1 < STAGES)(lambda: far(s + 1))
            if i == 17:
                pl.when(s + 1 < STAGES)(lambda: send_own(s + 1))

        t_buf[s] = combined_result(s)

        @pl.when(s < CHUNKS)
        def _():
            pltpu.make_async_copy(t_buf.at[s], out_one.at[:, columns], out_sem.at[s]).start()
            skeleton = make_message(s + CHUNKS, t_buf[s])
            upward(s + CHUNKS, skeleton)

        @pl.when(s >= CHUNKS)
        def _():
            t_buf[s] = 2.0 * t_buf[s] - v_buf[:, columns]
            pltpu.make_async_copy(t_buf.at[s], out_two.at[:, columns], out_sem.at[s]).start()

    for s in range(STAGES):
        columns = pl.ds((s % CHUNKS) * COLS, COLS)
        out = out_one if s < CHUNKS else out_two
        for half in range(2):
            wait_all(g.at[s, half, pl.ds(0, PEERS - 1)], g_send.at[s, half])
        wait_all(up_recv.at[s, pl.ds(1, PEERS - 1)], up_ss.at[s])
        wait_all(par.at[s, pl.ds(1, rows - 1)], row_ss.at[s])
        wait_all(far_recv.at[s, pl.ds(1, PEERS - 1)], far_ss.at[s])
        pltpu.make_async_copy(t_buf.at[s], out.at[:, columns], out_sem.at[s]).wait()


def local(
    probes,
    near_blocks,
    near_leaves,
    near_count,
    leaf_rank,
    leaf_basis,
    leaf_transfer,
    leaf_links,
    leaf_link_blocks,
    parent_links,
    parent_link_blocks,
):
    rows = lax.axis_size("row")
    smem = pl.BlockSpec(memory_space=pltpu.SMEM)
    hbm = pl.BlockSpec(memory_space=pl.ANY)
    dma = pltpu.SemaphoreType.DMA
    vmem = pltpu.VMEM
    folded = (2 * SHARE, PARENT // 2)
    return pl.pallas_call(
        functools.partial(kernel, rows),
        out_shape=[jax.ShapeDtypeStruct((LEAF, PROBES), F32)] * 2,
        in_specs=[smem] * 5 + [hbm] * 6,
        out_specs=[hbm] * 2,
        scratch_shapes=[
            vmem((STAGES, 2, PEERS, BLOCK, COLS), BF),
            vmem((8, LEAF, LEAF), BF),
            vmem((LEAF, PROBES), F32),
            vmem((LEAF, COLS), F32),
            vmem((RANK, COLS), F32),
            vmem((STAGES, LEAF, COLS), F32),
            vmem((LEAF, RANK), F32),
            vmem((RANK, PARENT), F32),
            vmem((4, RANK, RANK), F32),
            vmem((2, PARENT, PARENT), F32),
            vmem((LEAF, RANK), BF),
            vmem((LEAF, RANK), BF),
            vmem((RANK, LEAF), BF),
            vmem((RANK, LEAF), BF),
            vmem((RANK, PARENT), BF),
            vmem((4, RANK, RANK), BF),
            vmem((2, PARENT, PARENT), BF),
            vmem((STAGES, PEERS, *folded), BF),
            vmem((STAGES, PEERS, *folded), BF),
            vmem((STAGES, rows, *folded), BF),
            vmem((STAGES, PEERS, *folded), BF),
            *[pltpu.SMEM((PEERS,), jnp.int32)] * 4,
            dma((6,)),
            dma((STAGES,)),
            dma((STAGES, 2)),
            dma((STAGES, 2, PEERS)),
            *[dma((STAGES,))] * 6,
        ],
        compiler_params=pltpu.CompilerParams(
            collective_id=0, has_side_effects=True, vmem_limit_bytes=62 * 2**20
        ),
    )(
        near_leaves, near_count, leaf_rank, leaf_links, parent_links,
        probes, near_blocks, leaf_basis, leaf_transfer, leaf_link_blocks, parent_link_blocks,
    )


def solution(mesh):
    in_specs = (
        P(("row", "col"), None),
        P(("row", "col"), None, None, None),
        P(("row", "col"), None),
        P(("row", "col")),
        P(("row", "col")),
        P(("row", "col"), None),
        P(("row", "col"), None, None),
        P(("row", "col"), None),
        P(("row", "col"), None, None, None),
        P("row", None),
        P("row", None, None, None),
    )
    out_specs = (P(("row", "col"), None), P(("row", "col"), None))
    return jax.shard_map(local, mesh=mesh, in_specs=in_specs, out_specs=out_specs, check_vma=False)
```

```python
import functools

import jax
import jax.numpy as jnp
from jax import lax
from jax.experimental import pallas as pl
from jax.experimental.pallas import tpu as pltpu
from jax.sharding import PartitionSpec as P

BF = jnp.bfloat16
F32 = jnp.float32
SIDE = 4
PEERS = SIDE * SIDE
LEAF = 1024
HALF = LEAF // 2
RANK = 256
PARENT = 512
PROBES = 256
CHUNKS = 2
COLS = PROBES // CHUNKS
STAGES = 2 * CHUNKS
AHEAD = 8
BLOCK = HALF + RANK // 2
PIECE = BLOCK // 2
PARTS = 4
SHARE = PROBES // CHUNKS // PEERS


def dot(a, b, ca=1, cb=0):
    return lax.dot_general(a, b, (((ca,), (cb,)), ((), ())), preferred_element_type=F32)


def split(value):
    high = value.astype(BF)
    return high, (value - high.astype(F32)).astype(BF)


def dot_split(ah, al, bh, bl):
    return dot(ah, bh) + (dot(al, bh) + dot(ah, bl))


def fold(value):
    return jnp.concatenate([value[:, : PARENT // 2], value[:, PARENT // 2 :]], axis=0)


def unfold(value):
    return jnp.concatenate([value[:SHARE], value[SHARE:]], axis=1)


def kernel(
    rows,
    near_leaves, near_count, leaf_rank, leaf_links, parent_links,
    probes, near, basis, transfer, link_blocks, parent_blocks,
    out_one, out_two,
    g, near_buf, v_buf, acc, coup, t_buf,
    basis_f, transfer_f, link_f, parent_f,
    u_hi, u_lo, ut_hi, ut_lo, e_bf, l_bf, b_bf,
    up_send, up_recv, par, far_recv,
    near_slot, near_has, link_slot, link_has,
    load_sem, out_sem, g_send, g_recv, up_ss, up_rs, row_ss, row_rs, far_ss, far_rs,
):
    row = lax.axis_index("row")
    me = lax.axis_index("col")
    x, z = me // SIDE, me % SIDE

    loads = [
        pltpu.make_async_copy(src, dst, load_sem.at[i])
        for i, (src, dst) in enumerate(
            (
                (probes, v_buf),
                (basis, basis_f),
                (transfer.at[0], transfer_f),
                (link_blocks.at[0], link_f),
                (parent_blocks.at[0], parent_f),
                (near.at[0], near_buf),
            )
        )
    ]
    for load in loads[:2]:
        load.start()

    barrier = pltpu.get_barrier_semaphore()
    for d in range(1, PEERS):
        pl.semaphore_signal(barrier, inc=1, device_id={"col": (me + d) % PEERS})
    for d in range(1, rows):
        pl.semaphore_signal(barrier, inc=1, device_id={"row": (row + d) % rows})

    count = near_count[0]
    for a in range(SIDE):
        for b in range(SIDE):
            source = ((x + SIDE - a) % SIDE) * SIDE + (z + SIDE - b) % SIDE
            slot, has = jnp.int32(0), jnp.int32(0)
            for k in range(8):
                hit = jnp.logical_and(near_leaves[0, k] == source, k < count)
                slot, has = jnp.where(hit, k, slot), jnp.where(hit, 1, has)
            near_slot[a * SIDE + b] = slot
            near_has[a * SIDE + b] = has
            slot, has = jnp.int32(0), jnp.int32(0)
            for k in range(4):
                hit = leaf_links[0, k] == source
                slot, has = jnp.where(hit, k, slot), jnp.where(hit, 1, has)
            link_slot[a * SIDE + b] = slot
            link_has[a * SIDE + b] = has

    rank = leaf_rank[0]
    mask = lax.broadcasted_iota(jnp.int32, (RANK, COLS), 0) < rank

    def masked(value):
        return jnp.where(mask, value, jnp.zeros_like(value))

    def slot_of(half, p, q):
        return p * SIDE + q if half == 0 else q * SIDE + p

    def at_step(half, first, step):
        along_x = first == (half == 0)
        if along_x:
            return {"col": ((x + step + SIDE) % SIDE) * SIDE + z}
        return {"col": x * SIDE + (z + step + SIDE) % SIDE}

    def send(s, half, source, target, first, step, piece=None):
        src, dst = g.at[s, half, source], g.at[s, half, target]
        if piece is not None:
            part = pl.ds(piece * PIECE, PIECE)
            src, dst = src.at[part], dst.at[part]
        pltpu.make_async_remote_copy(
            src_ref=src,
            dst_ref=dst,
            send_sem=g_send.at[s, half],
            recv_sem=g_recv.at[s, half, target],
            device_id=at_step(half, first, step),
        ).start()

    def along_first(s, half, step, piece=None):
        source = slot_of(half, 0, 0) if piece is None else slot_of(half, step % SIDE, 0)
        target = slot_of(half, (step if piece is None else 2) % SIDE, 0)
        send(s, half, source, target, True, step, piece)

    def along_second(s, half, p, step, piece=None):
        source = slot_of(half, p, 0 if piece is None else step % SIDE)
        target = slot_of(half, p, (step if piece is None else 2) % SIDE)
        send(s, half, source, target, False, step, piece)

    def send_own(s):
        for half in range(2):
            for step in (1, -1):
                along_first(s, half, step)
            for step in (1, -1):
                along_second(s, half, 0, step)

    def arrive(s, half, p, q):
        slot = slot_of(half, p, q)
        ref = g.at[s, half, slot]
        pltpu.make_async_copy(ref, ref, g_recv.at[s, half, slot]).wait()
        if q == 0:
            if p == 1:
                along_first(s, half, 1, 0)
            if p == 3:
                along_first(s, half, -1, 1)
            along_second(s, half, p, 1)
            along_second(s, half, p, -1)
        elif q == 1:
            along_second(s, half, p, 1, 0)
        elif q == 3:
            along_second(s, half, p, -1, 1)

    def product(s, half, slot):
        block = g[s, half, slot, :HALF]
        block = jnp.where(near_has[slot] > 0, block, jnp.zeros_like(block))
        acc[s % 2] += dot(near_buf[near_slot[slot], :, half * HALF : (half + 1) * HALF], block)
        block = g[s, half, slot, HALF:]
        block = jnp.where(link_has[slot] > 0, block, jnp.zeros_like(block))
        width = RANK // 2
        coup[s % 2] += dot(l_bf[link_slot[slot], :, half * width : (half + 1) * width], block)

    def make_message(s, v):
        high, low = split(v)
        skeleton = masked(dot_split(ut_hi[...], ut_lo[...], high, low))
        packed = skeleton.astype(BF)
        for half in range(2):
            g[s, half, 0, :HALF] = high[half * HALF : (half + 1) * HALF]
            g[s, half, 0, HALF:] = packed[half * RANK // 2 : (half + 1) * RANK // 2]
        return skeleton

    def to_peers(src_of, dst_of, ss, rs):
        for d in range(1, PEERS):
            peer = (me + d) % PEERS
            pltpu.make_async_remote_copy(
                src_ref=src_of(peer), dst_ref=dst_of(d), send_sem=ss, recv_sem=rs, device_id={"col": peer}
            ).start()

    def upward(s, skeleton):
        up = dot(skeleton.T.astype(BF), e_bf[...])
        for j in range(PEERS):
            up_send[s, j] = fold(up[j * SHARE : (j + 1) * SHARE]).astype(BF)
        up_recv[s, 0] = up_send[s, me]
        to_peers(
            lambda peer: up_send.at[s, peer], lambda d: up_recv.at[s, d], up_ss.at[s], up_rs.at[s]
        )

    def wait_all(ref, sem):
        pltpu.make_async_copy(ref, ref, sem).wait()

    def parents(s):
        wait_all(up_recv.at[s, pl.ds(1, PEERS - 1)], up_rs.at[s])
        total = up_recv[s, 0].astype(F32)
        for d in range(1, PEERS):
            total += up_recv[s, d].astype(F32)
        par[s, 0] = total.astype(BF)
        for d in range(1, rows):
            pltpu.make_async_remote_copy(
                src_ref=par.at[s, 0],
                dst_ref=par.at[s, d],
                send_sem=row_ss.at[s],
                recv_sem=row_rs.at[s],
                device_id={"row": (row + d) % rows},
            ).start()

    def far(s):
        wait_all(par.at[s, pl.ds(1, rows - 1)], row_rs.at[s])
        total = jnp.zeros((SHARE, PARENT), F32)
        for k in range(2):
            away = (row + rows - parent_links[0, k]) % rows
            source = jnp.zeros((2 * SHARE, PARENT // 2), F32)
            for d in range(1, rows):
                source = jnp.where(away == d, par[s, d].astype(F32), source)
            source = source.astype(BF)
            total += dot(source, b_bf[k, :, : PARENT // 2], 1, 1)[:SHARE]
            total += dot(source, b_bf[k, :, PARENT // 2 :], 1, 1)[SHARE:]
        far_recv[s, me] = fold(total).astype(BF)
        to_peers(
            lambda peer: far_recv.at[s, me], lambda d: far_recv.at[s, me], far_ss.at[s], far_rs.at[s]
        )

    def combined_result(s):
        wait_all(far_recv.at[s, pl.ds(0, PEERS - 1)], far_rs.at[s])
        far_parent = jnp.concatenate(
            [unfold(far_recv[s, j].astype(F32)) for j in range(PEERS)], axis=0
        ).astype(BF)
        high, low = split(masked(coup[s % 2] + dot(e_bf[...], far_parent, 1, 1)))
        return dot_split(u_hi[...], u_lo[...], high, low) + acc[s % 2]

    loads[0].wait()
    loads[1].wait()
    for load in loads[2:]:
        load.start()
    u = basis_f[...]
    u_hi[...], u_lo[...] = split(u)
    ut_hi[...], ut_lo[...] = split(u.T)
    pl.semaphore_wait(barrier, PEERS - 1 + rows - 1)
    first = make_message(0, v_buf[:, :COLS])
    send_own(0)
    loads[2].wait()
    e_bf[...] = transfer_f[...].astype(BF)
    upward(0, first)
    for c in range(1, CHUNKS):
        upward(c, make_message(c, v_buf[:, c * COLS : (c + 1) * COLS]))
    loads[3].wait()
    l_bf[...] = link_f[...].astype(BF)
    loads[4].wait()
    b_bf[...] = parent_f[...].astype(BF)
    loads[5].wait()

    events = [(1, 0), (3, 0), (0, 1), (0, 3), (2, 0)]
    events += [(p, q) for p in (1, 3, 2) for q in (1, 3)]
    events += [(0, 2), (1, 2), (3, 2), (2, 2)]
    events = [(half, p, q) for p, q in events for half in range(2)]

    def finish(s):
        columns = pl.ds(pl.multiple_of((s % CHUNKS) * COLS, COLS), COLS)
        t_buf[s] = combined_result(s)

        @pl.when(s < CHUNKS)
        def _():
            pltpu.make_async_copy(t_buf.at[s], out_one.at[:, columns], out_sem.at[s]).start()
            upward(s + CHUNKS, make_message(s + CHUNKS, t_buf[s]))

        @pl.when(s >= CHUNKS)
        def _():
            t_buf[s] = 2.0 * t_buf[s] - v_buf[:, columns]
            pltpu.make_async_copy(t_buf.at[s], out_two.at[:, columns], out_sem.at[s]).start()

    @pl.loop(0, STAGES)
    def _(s):
        acc[s % 2] = jnp.zeros((LEAF, COLS), F32)
        coup[s % 2] = jnp.zeros((RANK, COLS), F32)
        for half in range(2):
            product(s, half, 0)
        for i, (half, p, q) in enumerate(events):
            if i < AHEAD:
                pl.when(s == 0)(lambda: arrive(s, half, p, q))
            else:
                arrive(s, half, p, q)
            if i == 11:
                pl.when(s == 0)(lambda: parents(0))
            if i == 23:
                pl.when(s == 0)(lambda: far(0))
            if i == 23:
                pl.when(s + 1 < STAGES)(lambda: parents(s + 1))
            if i == 3:
                pl.when(s > 0)(lambda: far(s))
            if i == 13:
                pl.when(s > 0)(lambda: finish(s - 1))
            if i == 17:
                pl.when(s + 1 < STAGES)(lambda: send_own(s + 1))
            if i == 27:

                @pl.when(s + 1 < STAGES)
                def _():
                    for event in events[:AHEAD]:
                        arrive(s + 1, *event)

            product(s, half, slot_of(half, p, q))

    finish(STAGES - 1)

    for s in range(STAGES):
        columns = pl.ds((s % CHUNKS) * COLS, COLS)
        out = out_one if s < CHUNKS else out_two
        for half in range(2):
            wait_all(g.at[s, half, pl.ds(0, PEERS - 1)], g_send.at[s, half])
        wait_all(up_recv.at[s, pl.ds(1, PEERS - 1)], up_ss.at[s])
        wait_all(par.at[s, pl.ds(1, rows - 1)], row_ss.at[s])
        wait_all(far_recv.at[s, pl.ds(1, PEERS - 1)], far_ss.at[s])
        pltpu.make_async_copy(t_buf.at[s], out.at[:, columns], out_sem.at[s]).wait()


def hand_on(one, two, out_one, out_two):
    out_one[...] = one[...]
    out_two[...] = two[...]


def local(
    probes,
    near_blocks,
    near_leaves,
    near_count,
    leaf_rank,
    leaf_basis,
    leaf_transfer,
    leaf_links,
    leaf_link_blocks,
    parent_links,
    parent_link_blocks,
):
    rows = lax.axis_size("row")
    smem = pl.BlockSpec(memory_space=pltpu.SMEM)
    hbm = pl.BlockSpec(memory_space=pl.ANY)
    dma = pltpu.SemaphoreType.DMA
    vmem = pltpu.VMEM
    folded = (2 * SHARE, PARENT // 2)
    terms = pl.pallas_call(
        functools.partial(kernel, rows),
        out_shape=[jax.ShapeDtypeStruct((LEAF, PROBES), F32)] * 2,
        in_specs=[smem] * 5 + [hbm] * 6,
        out_specs=[hbm] * 2,
        scratch_shapes=[
            vmem((STAGES, 2, PEERS, BLOCK, COLS), BF),
            vmem((8, LEAF, LEAF), BF),
            vmem((LEAF, PROBES), F32),
            vmem((2, LEAF, COLS), F32),
            vmem((2, RANK, COLS), F32),
            vmem((STAGES, LEAF, COLS), F32),
            vmem((LEAF, RANK), F32),
            vmem((RANK, PARENT), F32),
            vmem((4, RANK, RANK), F32),
            vmem((2, PARENT, PARENT), F32),
            vmem((LEAF, RANK), BF),
            vmem((LEAF, RANK), BF),
            vmem((RANK, LEAF), BF),
            vmem((RANK, LEAF), BF),
            vmem((RANK, PARENT), BF),
            vmem((4, RANK, RANK), BF),
            vmem((2, PARENT, PARENT), BF),
            vmem((STAGES, PEERS, *folded), BF),
            vmem((STAGES, PEERS, *folded), BF),
            vmem((STAGES, rows, *folded), BF),
            vmem((STAGES, PEERS, *folded), BF),
            *[pltpu.SMEM((PEERS,), jnp.int32)] * 4,
            dma((6,)),
            dma((STAGES,)),
            dma((STAGES, 2)),
            dma((STAGES, 2, PEERS)),
            *[dma((STAGES,))] * 6,
        ],
        compiler_params=pltpu.CompilerParams(
            collective_id=0, has_side_effects=True, vmem_limit_bytes=62 * 2**20
        ),
    )(
        near_leaves, near_count, leaf_rank, leaf_links, parent_links,
        probes, near_blocks, leaf_basis, leaf_transfer, leaf_link_blocks, parent_link_blocks,
    )
    part = pl.BlockSpec((LEAF // PARTS, PROBES), lambda i: (i, 0))
    return pl.pallas_call(
        hand_on,
        grid=(PARTS,),
        out_shape=[jax.ShapeDtypeStruct((LEAF, PROBES), F32)] * 2,
        in_specs=[part] * 2,
        out_specs=[part] * 2,
    )(*terms)


def solution(mesh):
    in_specs = (
        P(("row", "col"), None),
        P(("row", "col"), None, None, None),
        P(("row", "col"), None),
        P(("row", "col")),
        P(("row", "col")),
        P(("row", "col"), None),
        P(("row", "col"), None, None),
        P(("row", "col"), None),
        P(("row", "col"), None, None, None),
        P("row", None),
        P("row", None, None, None),
    )
    out_specs = (P(("row", "col"), None), P(("row", "col"), None))
    return jax.shard_map(local, mesh=mesh, in_specs=in_specs, out_specs=out_specs, check_vma=False)
```

```python
import functools

import jax
import jax.numpy as jnp
from jax import lax
from jax.experimental import pallas as pl
from jax.experimental.pallas import tpu as pltpu
from jax.sharding import PartitionSpec as P

BF = jnp.bfloat16
F32 = jnp.float32
SIDE = 4
PEERS = SIDE * SIDE
LEAF = 1024
HALF = LEAF // 2
RANK = 256
PARENT = 512
PROBES = 256
CHUNKS = 2
COLS = PROBES // CHUNKS
STAGES = 2 * CHUNKS
AHEAD = 4
BLOCK = HALF + RANK // 2
PIECE = BLOCK // 2
PARTS = 2
SHARE = PROBES // CHUNKS // PEERS


def dot(a, b, ca=1, cb=0):
    return lax.dot_general(a, b, (((ca,), (cb,)), ((), ())), preferred_element_type=F32)


def split(value):
    high = value.astype(BF)
    return high, (value - high.astype(F32)).astype(BF)


def dot_split(ah, al, bh, bl):
    return dot(ah, bh) + (dot(al, bh) + dot(ah, bl))


def fold(value):
    return jnp.concatenate([value[:, : PARENT // 2], value[:, PARENT // 2 :]], axis=0)


def unfold(value):
    return jnp.concatenate([value[:SHARE], value[SHARE:]], axis=1)


def kernel(
    rows,
    near_leaves, near_count, leaf_rank, leaf_links, parent_links,
    probes, near, basis, transfer, link_blocks, parent_blocks,
    out_one, out_two,
    g, near_buf, v_buf, acc, coup, t_buf,
    basis_f, transfer_f, link_f, parent_f,
    u_hi, u_lo, ut_hi, ut_lo, e_bf, l_bf, b_bf,
    up_send, up_recv, par, far_recv,
    near_slot, near_has, link_slot, link_has,
    load_sem, out_sem, g_send, g_recv, up_ss, up_rs, row_ss, row_rs, far_ss, far_rs,
):
    row = lax.axis_index("row")
    me = lax.axis_index("col")
    x, z = me // SIDE, me % SIDE

    loads = [
        pltpu.make_async_copy(src, dst, load_sem.at[i])
        for i, (src, dst) in enumerate(
            (
                (probes, v_buf),
                (basis, basis_f),
                (transfer.at[0], transfer_f),
                (link_blocks.at[0], link_f),
                (parent_blocks.at[0], parent_f),
                (near.at[0], near_buf),
            )
        )
    ]
    for load in loads[:2]:
        load.start()

    barrier = pltpu.get_barrier_semaphore()
    for d in range(1, PEERS):
        pl.semaphore_signal(barrier, inc=1, device_id={"col": (me + d) % PEERS})
    for d in range(1, rows):
        pl.semaphore_signal(barrier, inc=1, device_id={"row": (row + d) % rows})

    count = near_count[0]
    for a in range(SIDE):
        for b in range(SIDE):
            source = ((x + SIDE - a) % SIDE) * SIDE + (z + SIDE - b) % SIDE
            slot, has = jnp.int32(0), jnp.int32(0)
            for k in range(8):
                hit = jnp.logical_and(near_leaves[0, k] == source, k < count)
                slot, has = jnp.where(hit, k, slot), jnp.where(hit, 1, has)
            near_slot[a * SIDE + b] = slot
            near_has[a * SIDE + b] = has
            slot, has = jnp.int32(0), jnp.int32(0)
            for k in range(4):
                hit = leaf_links[0, k] == source
                slot, has = jnp.where(hit, k, slot), jnp.where(hit, 1, has)
            link_slot[a * SIDE + b] = slot
            link_has[a * SIDE + b] = has

    rank = leaf_rank[0]
    mask = lax.broadcasted_iota(jnp.int32, (RANK, COLS), 0) < rank

    def masked(value):
        return jnp.where(mask, value, jnp.zeros_like(value))

    def slot_of(half, p, q):
        return p * SIDE + q if half == 0 else q * SIDE + p

    def at_step(half, first, step):
        along_x = first == (half == 0)
        if along_x:
            return {"col": ((x + step + SIDE) % SIDE) * SIDE + z}
        return {"col": x * SIDE + (z + step + SIDE) % SIDE}

    def send(s, half, source, target, first, step, piece=None):
        src, dst = g.at[s, half, source], g.at[s, half, target]
        if piece is not None:
            part = pl.ds(piece * PIECE, PIECE)
            src, dst = src.at[part], dst.at[part]
        pltpu.make_async_remote_copy(
            src_ref=src,
            dst_ref=dst,
            send_sem=g_send.at[s, half],
            recv_sem=g_recv.at[s, half, target],
            device_id=at_step(half, first, step),
        ).start()

    def along_first(s, half, step, piece=None):
        source = slot_of(half, 0, 0) if piece is None else slot_of(half, step % SIDE, 0)
        target = slot_of(half, (step if piece is None else 2) % SIDE, 0)
        send(s, half, source, target, True, step, piece)

    def along_second(s, half, p, step, piece=None):
        source = slot_of(half, p, 0 if piece is None else step % SIDE)
        target = slot_of(half, p, (step if piece is None else 2) % SIDE)
        send(s, half, source, target, False, step, piece)

    def send_own(s):
        for half in range(2):
            for step in (1, -1):
                along_first(s, half, step)
            for step in (1, -1):
                along_second(s, half, 0, step)

    def arrive(s, half, p, q):
        slot = slot_of(half, p, q)
        ref = g.at[s, half, slot]
        pltpu.make_async_copy(ref, ref, g_recv.at[s, half, slot]).wait()
        if q == 0:
            if p == 1:
                along_first(s, half, 1, 0)
            if p == 3:
                along_first(s, half, -1, 1)
            along_second(s, half, p, 1)
            along_second(s, half, p, -1)
        elif q == 1:
            along_second(s, half, p, 1, 0)
        elif q == 3:
            along_second(s, half, p, -1, 1)

    def product(s, half, slot):
        block = g[s, half, slot, :HALF]
        block = jnp.where(near_has[slot] > 0, block, jnp.zeros_like(block))
        acc[s % 2] += dot(near_buf[near_slot[slot], :, half * HALF : (half + 1) * HALF], block)
        block = g[s, half, slot, HALF:]
        block = jnp.where(link_has[slot] > 0, block, jnp.zeros_like(block))
        width = RANK // 2
        coup[s % 2] += dot(l_bf[link_slot[slot], :, half * width : (half + 1) * width], block)

    def make_message(s, v):
        high, low = split(v)
        skeleton = masked(dot_split(ut_hi[...], ut_lo[...], high, low))
        packed = skeleton.astype(BF)
        for half in range(2):
            g[s, half, 0, :HALF] = high[half * HALF : (half + 1) * HALF]
            g[s, half, 0, HALF:] = packed[half * RANK // 2 : (half + 1) * RANK // 2]
        return skeleton

    def to_peers(src_of, dst_of, ss, rs):
        for d in range(1, PEERS):
            peer = (me + d) % PEERS
            pltpu.make_async_remote_copy(
                src_ref=src_of(peer), dst_ref=dst_of(d), send_sem=ss, recv_sem=rs, device_id={"col": peer}
            ).start()

    def upward(s, skeleton):
        up = dot(skeleton.T.astype(BF), e_bf[...])
        for j in range(PEERS):
            up_send[s, j] = fold(up[j * SHARE : (j + 1) * SHARE]).astype(BF)
        up_recv[s, 0] = up_send[s, me]
        to_peers(
            lambda peer: up_send.at[s, peer], lambda d: up_recv.at[s, d], up_ss.at[s], up_rs.at[s]
        )

    def wait_all(ref, sem):
        pltpu.make_async_copy(ref, ref, sem).wait()

    def parents(s):
        wait_all(up_recv.at[s, pl.ds(1, PEERS - 1)], up_rs.at[s])
        total = up_recv[s, 0].astype(F32)
        for d in range(1, PEERS):
            total += up_recv[s, d].astype(F32)
        par[s, 0] = total.astype(BF)
        for d in range(1, rows):
            pltpu.make_async_remote_copy(
                src_ref=par.at[s, 0],
                dst_ref=par.at[s, d],
                send_sem=row_ss.at[s],
                recv_sem=row_rs.at[s],
                device_id={"row": (row + d) % rows},
            ).start()

    def far(s):
        wait_all(par.at[s, pl.ds(1, rows - 1)], row_rs.at[s])
        total = jnp.zeros((SHARE, PARENT), F32)
        for k in range(2):
            away = (row + rows - parent_links[0, k]) % rows
            source = jnp.zeros((2 * SHARE, PARENT // 2), F32)
            for d in range(1, rows):
                source = jnp.where(away == d, par[s, d].astype(F32), source)
            source = source.astype(BF)
            total += dot(source, b_bf[k, :, : PARENT // 2], 1, 1)[:SHARE]
            total += dot(source, b_bf[k, :, PARENT // 2 :], 1, 1)[SHARE:]
        far_recv[s, me] = fold(total).astype(BF)
        to_peers(
            lambda peer: far_recv.at[s, me], lambda d: far_recv.at[s, me], far_ss.at[s], far_rs.at[s]
        )

    def combined_result(s):
        wait_all(far_recv.at[s, pl.ds(0, PEERS - 1)], far_rs.at[s])
        far_parent = jnp.concatenate(
            [unfold(far_recv[s, j].astype(F32)) for j in range(PEERS)], axis=0
        ).astype(BF)
        high, low = split(masked(coup[s % 2] + dot(e_bf[...], far_parent, 1, 1)))
        return dot_split(u_hi[...], u_lo[...], high, low) + acc[s % 2]

    loads[0].wait()
    loads[1].wait()
    for load in loads[2:]:
        load.start()
    u = basis_f[...]
    u_hi[...], u_lo[...] = split(u)
    ut_hi[...], ut_lo[...] = split(u.T)
    pl.semaphore_wait(barrier, PEERS - 1 + rows - 1)
    first = make_message(0, v_buf[:, :COLS])
    send_own(0)
    loads[2].wait()
    e_bf[...] = transfer_f[...].astype(BF)
    upward(0, first)
    for c in range(1, CHUNKS):
        upward(c, make_message(c, v_buf[:, c * COLS : (c + 1) * COLS]))
    loads[3].wait()
    l_bf[...] = link_f[...].astype(BF)
    loads[4].wait()
    b_bf[...] = parent_f[...].astype(BF)
    loads[5].wait()

    events = [(1, 0), (3, 0), (0, 1), (0, 3), (2, 0)]
    events += [(p, q) for p in (1, 3, 2) for q in (1, 3)]
    events += [(0, 2), (1, 2), (3, 2), (2, 2)]
    events = [(half, p, q) for p, q in events for half in range(2)]

    def finish(s):
        columns = pl.ds(pl.multiple_of((s % CHUNKS) * COLS, COLS), COLS)
        t_buf[s] = combined_result(s)

        @pl.when(s < CHUNKS)
        def _():
            pltpu.make_async_copy(t_buf.at[s], out_one.at[:, columns], out_sem.at[s]).start()
            upward(s + CHUNKS, make_message(s + CHUNKS, t_buf[s]))

        @pl.when(s >= CHUNKS)
        def _():
            t_buf[s] = 2.0 * t_buf[s] - v_buf[:, columns]
            pltpu.make_async_copy(t_buf.at[s], out_two.at[:, columns], out_sem.at[s]).start()

    @pl.loop(0, STAGES)
    def _(s):
        acc[s % 2] = jnp.zeros((LEAF, COLS), F32)
        coup[s % 2] = jnp.zeros((RANK, COLS), F32)
        for half in range(2):
            product(s, half, 0)
        for i, (half, p, q) in enumerate(events):
            if i < AHEAD:
                pl.when(s == 0)(lambda: arrive(s, half, p, q))
            else:
                arrive(s, half, p, q)
            if i == 11:
                pl.when(s == 0)(lambda: parents(0))
            if i == 23:
                pl.when(s == 0)(lambda: far(0))
            if i == 23:
                pl.when(s + 1 < STAGES)(lambda: parents(s + 1))
            if i == 3:
                pl.when(s > 0)(lambda: far(s))
            if i == 13:
                pl.when(s > 0)(lambda: finish(s - 1))
            if i == 17:
                pl.when(s + 1 < STAGES)(lambda: send_own(s + 1))
            if i == 27:

                @pl.when(s + 1 < STAGES)
                def _():
                    for event in events[:AHEAD]:
                        arrive(s + 1, *event)

            product(s, half, slot_of(half, p, q))

    finish(STAGES - 1)

    for s in range(STAGES):
        columns = pl.ds((s % CHUNKS) * COLS, COLS)
        out = out_one if s < CHUNKS else out_two
        for half in range(2):
            wait_all(g.at[s, half, pl.ds(0, PEERS - 1)], g_send.at[s, half])
        wait_all(up_recv.at[s, pl.ds(1, PEERS - 1)], up_ss.at[s])
        wait_all(par.at[s, pl.ds(1, rows - 1)], row_ss.at[s])
        wait_all(far_recv.at[s, pl.ds(1, PEERS - 1)], far_ss.at[s])
        pltpu.make_async_copy(t_buf.at[s], out.at[:, columns], out_sem.at[s]).wait()


def hand_on(one, two, out_one, out_two, held, sem):
    rows = LEAF // PARTS
    steps = []
    for i, (src, dst) in enumerate(((one, out_one), (two, out_two))):
        for j in range(PARTS):
            part = pl.ds(j * rows, rows)
            steps.append(
                (
                    pltpu.make_async_copy(src.at[part], held.at[i, part], sem.at[0, i, j]),
                    pltpu.make_async_copy(held.at[i, part], dst.at[part], sem.at[1, i, j]),
                )
            )
    for come, _ in steps:
        come.start()
    for come, go in steps:
        come.wait()
        go.start()
    for _, go in steps:
        go.wait()


def local(
    probes,
    near_blocks,
    near_leaves,
    near_count,
    leaf_rank,
    leaf_basis,
    leaf_transfer,
    leaf_links,
    leaf_link_blocks,
    parent_links,
    parent_link_blocks,
):
    rows = lax.axis_size("row")
    smem = pl.BlockSpec(memory_space=pltpu.SMEM)
    hbm = pl.BlockSpec(memory_space=pl.ANY)
    dma = pltpu.SemaphoreType.DMA
    vmem = pltpu.VMEM
    folded = (2 * SHARE, PARENT // 2)
    terms = pl.pallas_call(
        functools.partial(kernel, rows),
        out_shape=[jax.ShapeDtypeStruct((LEAF, PROBES), F32)] * 2,
        in_specs=[smem] * 5 + [hbm] * 6,
        out_specs=[hbm] * 2,
        scratch_shapes=[
            vmem((STAGES, 2, PEERS, BLOCK, COLS), BF),
            vmem((8, LEAF, LEAF), BF),
            vmem((LEAF, PROBES), F32),
            vmem((2, LEAF, COLS), F32),
            vmem((2, RANK, COLS), F32),
            vmem((STAGES, LEAF, COLS), F32),
            vmem((LEAF, RANK), F32),
            vmem((RANK, PARENT), F32),
            vmem((4, RANK, RANK), F32),
            vmem((2, PARENT, PARENT), F32),
            vmem((LEAF, RANK), BF),
            vmem((LEAF, RANK), BF),
            vmem((RANK, LEAF), BF),
            vmem((RANK, LEAF), BF),
            vmem((RANK, PARENT), BF),
            vmem((4, RANK, RANK), BF),
            vmem((2, PARENT, PARENT), BF),
            vmem((STAGES, PEERS, *folded), BF),
            vmem((STAGES, PEERS, *folded), BF),
            vmem((STAGES, rows, *folded), BF),
            vmem((STAGES, PEERS, *folded), BF),
            *[pltpu.SMEM((PEERS,), jnp.int32)] * 4,
            dma((6,)),
            dma((STAGES,)),
            dma((STAGES, 2)),
            dma((STAGES, 2, PEERS)),
            *[dma((STAGES,))] * 6,
        ],
        compiler_params=pltpu.CompilerParams(
            collective_id=0, has_side_effects=True, vmem_limit_bytes=62 * 2**20
        ),
    )(
        near_leaves, near_count, leaf_rank, leaf_links, parent_links,
        probes, near_blocks, leaf_basis, leaf_transfer, leaf_link_blocks, parent_link_blocks,
    )
    return pl.pallas_call(
        hand_on,
        out_shape=[jax.ShapeDtypeStruct((LEAF, PROBES), F32)] * 2,
        in_specs=[hbm] * 2,
        out_specs=[hbm] * 2,
        scratch_shapes=[vmem((2, LEAF, PROBES), F32), dma((2, 2, PARTS))],
    )(*terms)


def solution(mesh):
    in_specs = (
        P(("row", "col"), None),
        P(("row", "col"), None, None, None),
        P(("row", "col"), None),
        P(("row", "col")),
        P(("row", "col")),
        P(("row", "col"), None),
        P(("row", "col"), None, None),
        P(("row", "col"), None),
        P(("row", "col"), None, None, None),
        P("row", None),
        P("row", None, None, None),
    )
    out_specs = (P(("row", "col"), None), P(("row", "col"), None))
    return jax.shard_map(local, mesh=mesh, in_specs=in_specs, out_specs=out_specs, check_vma=False)
```

```python
import functools

import jax
import jax.numpy as jnp
from jax import lax
from jax.experimental import pallas as pl
from jax.experimental.pallas import tpu as pltpu
from jax.sharding import PartitionSpec as P

BF = jnp.bfloat16
F32 = jnp.float32
SIDE = 4
PEERS = SIDE * SIDE
LEAF = 1024
HALF = LEAF // 2
RANK = 256
PARENT = 512
PROBES = 256
CHUNKS = 2
COLS = PROBES // CHUNKS
STAGES = 2 * CHUNKS
AHEAD = 4
BLOCK = HALF + RANK // 2
PIECE = BLOCK // 2
PARTS = 2
SHARE = PROBES // CHUNKS // PEERS


def dot(a, b, ca=1, cb=0):
    return lax.dot_general(a, b, (((ca,), (cb,)), ((), ())), preferred_element_type=F32)


def split(value):
    high = value.astype(BF)
    return high, (value - high.astype(F32)).astype(BF)


def dot_split(ah, al, bh, bl):
    return dot(ah, bh) + (dot(al, bh) + dot(ah, bl))


def fold(value):
    return jnp.concatenate([value[:, : PARENT // 2], value[:, PARENT // 2 :]], axis=0)


def unfold(value):
    return jnp.concatenate([value[:SHARE], value[SHARE:]], axis=1)


def kernel(
    rows,
    near_leaves, near_count, leaf_rank, leaf_links, parent_links,
    probes, near, basis, transfer, link_blocks, parent_blocks,
    out_one, out_two,
    g, near_buf, v_buf, acc, coup, t_buf,
    basis_f, transfer_f, link_f, parent_f,
    u_hi, u_lo, ut_hi, ut_lo, e_bf, l_bf, b_bf,
    up_send, up_recv, par, far_recv,
    near_slot, near_has, link_slot, link_has,
    load_sem, out_sem, g_send, g_recv, up_ss, up_rs, row_ss, row_rs, far_ss, far_rs,
):
    row = lax.axis_index("row")
    me = lax.axis_index("col")
    x, z = me // SIDE, me % SIDE

    loads = [
        pltpu.make_async_copy(src, dst, load_sem.at[i])
        for i, (src, dst) in enumerate(
            (
                (probes, v_buf),
                (basis, basis_f),
                (transfer.at[0], transfer_f),
                (link_blocks.at[0], link_f),
                (parent_blocks.at[0], parent_f),
                (near.at[0], near_buf),
            )
        )
    ]
    for load in loads[:2]:
        load.start()

    barrier = pltpu.get_barrier_semaphore()
    for d in range(1, PEERS):
        pl.semaphore_signal(barrier, inc=1, device_id={"col": (me + d) % PEERS})
    for d in range(1, rows):
        pl.semaphore_signal(barrier, inc=1, device_id={"row": (row + d) % rows})

    count = near_count[0]
    for a in range(SIDE):
        for b in range(SIDE):
            source = ((x + SIDE - a) % SIDE) * SIDE + (z + SIDE - b) % SIDE
            slot, has = jnp.int32(0), jnp.int32(0)
            for k in range(8):
                hit = jnp.logical_and(near_leaves[0, k] == source, k < count)
                slot, has = jnp.where(hit, k, slot), jnp.where(hit, 1, has)
            near_slot[a * SIDE + b] = slot
            near_has[a * SIDE + b] = has
            slot, has = jnp.int32(0), jnp.int32(0)
            for k in range(4):
                hit = leaf_links[0, k] == source
                slot, has = jnp.where(hit, k, slot), jnp.where(hit, 1, has)
            link_slot[a * SIDE + b] = slot
            link_has[a * SIDE + b] = has

    rank = leaf_rank[0]
    mask = lax.broadcasted_iota(jnp.int32, (RANK, COLS), 0) < rank

    def masked(value):
        return jnp.where(mask, value, jnp.zeros_like(value))

    def slot_of(half, p, q):
        return p * SIDE + q if half == 0 else q * SIDE + p

    def at_step(half, first, step):
        along_x = first == (half == 0)
        if along_x:
            return {"col": ((x + step + SIDE) % SIDE) * SIDE + z}
        return {"col": x * SIDE + (z + step + SIDE) % SIDE}

    def send(s, half, source, target, first, step, piece=None):
        src, dst = g.at[s, half, source], g.at[s, half, target]
        if piece is not None:
            part = pl.ds(piece * PIECE, PIECE)
            src, dst = src.at[part], dst.at[part]
        pltpu.make_async_remote_copy(
            src_ref=src,
            dst_ref=dst,
            send_sem=g_send.at[s, half],
            recv_sem=g_recv.at[s, half, target],
            device_id=at_step(half, first, step),
        ).start()

    def along_first(s, half, step, piece=None):
        source = slot_of(half, 0, 0) if piece is None else slot_of(half, step % SIDE, 0)
        target = slot_of(half, (step if piece is None else 2) % SIDE, 0)
        send(s, half, source, target, True, step, piece)

    def along_second(s, half, p, step, piece=None):
        source = slot_of(half, p, 0 if piece is None else step % SIDE)
        target = slot_of(half, p, (step if piece is None else 2) % SIDE)
        send(s, half, source, target, False, step, piece)

    def send_own(s):
        for half in range(2):
            for step in (1, -1):
                along_first(s, half, step)
            for step in (1, -1):
                along_second(s, half, 0, step)

    def arrive(s, half, p, q):
        slot = slot_of(half, p, q)
        ref = g.at[s, half, slot]
        pltpu.make_async_copy(ref, ref, g_recv.at[s, half, slot]).wait()
        if q == 0:
            if p == 1:
                along_first(s, half, 1, 0)
            if p == 3:
                along_first(s, half, -1, 1)
            along_second(s, half, p, 1)
            along_second(s, half, p, -1)
        elif q == 1:
            along_second(s, half, p, 1, 0)
        elif q == 3:
            along_second(s, half, p, -1, 1)

    def product(s, half, slot):
        block = g[s, half, slot, :HALF]
        block = jnp.where(near_has[slot] > 0, block, jnp.zeros_like(block))
        acc[s % 2] += dot(near_buf[near_slot[slot], :, half * HALF : (half + 1) * HALF], block)
        block = g[s, half, slot, HALF:]
        block = jnp.where(link_has[slot] > 0, block, jnp.zeros_like(block))
        width = RANK // 2
        coup[s % 2] += dot(l_bf[link_slot[slot], :, half * width : (half + 1) * width], block)

    def make_message(s, v):
        high, low = split(v)
        skeleton = masked(dot_split(ut_hi[...], ut_lo[...], high, low))
        packed = skeleton.astype(BF)
        for half in range(2):
            g[s, half, 0, :HALF] = high[half * HALF : (half + 1) * HALF]
            g[s, half, 0, HALF:] = packed[half * RANK // 2 : (half + 1) * RANK // 2]
        return skeleton

    def to_peers(src_of, dst_of, ss, rs):
        for d in (1, 15, 4, 12, 3, 13, 5, 11, 2, 14, 8, 7, 9, 6, 10):
            peer = (me + d) % PEERS
            pltpu.make_async_remote_copy(
                src_ref=src_of(peer), dst_ref=dst_of(d), send_sem=ss, recv_sem=rs, device_id={"col": peer}
            ).start()

    def upward(s, skeleton):
        up = dot(skeleton.T.astype(BF), e_bf[...])
        for j in range(PEERS):
            up_send[s, j] = fold(up[j * SHARE : (j + 1) * SHARE]).astype(BF)
        up_recv[s, 0] = up_send[s, me]
        to_peers(
            lambda peer: up_send.at[s, peer], lambda d: up_recv.at[s, d], up_ss.at[s], up_rs.at[s]
        )

    def wait_all(ref, sem):
        pltpu.make_async_copy(ref, ref, sem).wait()

    def parents(s):
        wait_all(up_recv.at[s, pl.ds(1, PEERS - 1)], up_rs.at[s])
        total = up_recv[s, 0].astype(F32)
        for d in range(1, PEERS):
            total += up_recv[s, d].astype(F32)
        par[s, 0] = total.astype(BF)
        for d in range(1, rows):
            pltpu.make_async_remote_copy(
                src_ref=par.at[s, 0],
                dst_ref=par.at[s, d],
                send_sem=row_ss.at[s],
                recv_sem=row_rs.at[s],
                device_id={"row": (row + d) % rows},
            ).start()

    def far(s):
        wait_all(par.at[s, pl.ds(1, rows - 1)], row_rs.at[s])
        total = jnp.zeros((SHARE, PARENT), F32)
        for k in range(2):
            away = (row + rows - parent_links[0, k]) % rows
            source = jnp.zeros((2 * SHARE, PARENT // 2), F32)
            for d in range(1, rows):
                source = jnp.where(away == d, par[s, d].astype(F32), source)
            source = source.astype(BF)
            total += dot(source, b_bf[k, :, : PARENT // 2], 1, 1)[:SHARE]
            total += dot(source, b_bf[k, :, PARENT // 2 :], 1, 1)[SHARE:]
        far_recv[s, me] = fold(total).astype(BF)
        to_peers(
            lambda peer: far_recv.at[s, me], lambda d: far_recv.at[s, me], far_ss.at[s], far_rs.at[s]
        )

    def combined_result(s):
        wait_all(far_recv.at[s, pl.ds(0, PEERS - 1)], far_rs.at[s])
        far_parent = jnp.concatenate(
            [unfold(far_recv[s, j].astype(F32)) for j in range(PEERS)], axis=0
        ).astype(BF)
        high, low = split(masked(coup[s % 2] + dot(e_bf[...], far_parent, 1, 1)))
        return dot_split(u_hi[...], u_lo[...], high, low) + acc[s % 2]

    loads[0].wait()
    loads[1].wait()
    for load in loads[2:]:
        load.start()
    u = basis_f[...]
    u_hi[...], u_lo[...] = split(u)
    ut_hi[...], ut_lo[...] = split(u.T)
    pl.semaphore_wait(barrier, PEERS - 1 + rows - 1)
    first = make_message(0, v_buf[:, :COLS])
    send_own(0)
    loads[2].wait()
    e_bf[...] = transfer_f[...].astype(BF)
    upward(0, first)
    for c in range(1, CHUNKS):
        upward(c, make_message(c, v_buf[:, c * COLS : (c + 1) * COLS]))
    loads[3].wait()
    l_bf[...] = link_f[...].astype(BF)
    loads[4].wait()
    b_bf[...] = parent_f[...].astype(BF)
    loads[5].wait()

    events = [(1, 0), (3, 0), (0, 1), (0, 3), (2, 0)]
    events += [(p, q) for p in (1, 3, 2) for q in (1, 3)]
    events += [(0, 2), (1, 2), (3, 2), (2, 2)]
    events = [(half, p, q) for p, q in events for half in range(2)]

    def finish(s):
        columns = pl.ds(pl.multiple_of((s % CHUNKS) * COLS, COLS), COLS)
        t_buf[s] = combined_result(s)

        @pl.when(s < CHUNKS)
        def _():
            pltpu.make_async_copy(t_buf.at[s], out_one.at[:, columns], out_sem.at[s]).start()
            upward(s + CHUNKS, make_message(s + CHUNKS, t_buf[s]))

        @pl.when(s >= CHUNKS)
        def _():
            t_buf[s] = 2.0 * t_buf[s] - v_buf[:, columns]
            pltpu.make_async_copy(t_buf.at[s], out_two.at[:, columns], out_sem.at[s]).start()

    @pl.loop(0, STAGES)
    def _(s):
        acc[s % 2] = jnp.zeros((LEAF, COLS), F32)
        coup[s % 2] = jnp.zeros((RANK, COLS), F32)
        for half in range(2):
            product(s, half, 0)
        for i, (half, p, q) in enumerate(events):
            if i < AHEAD:
                pl.when(s == 0)(lambda: arrive(s, half, p, q))
            else:
                arrive(s, half, p, q)
            if i == 11:
                pl.when(s == 0)(lambda: parents(0))
            if i == 23:
                pl.when(s == 0)(lambda: far(0))
            if i == 23:
                pl.when(s + 1 < STAGES)(lambda: parents(s + 1))
            if i == 3:
                pl.when(s > 0)(lambda: far(s))
            if i == 13:
                pl.when(s > 0)(lambda: finish(s - 1))
            if i == 17:
                pl.when(s + 1 < STAGES)(lambda: send_own(s + 1))
            if i == 27:

                @pl.when(s + 1 < STAGES)
                def _():
                    for event in events[:AHEAD]:
                        arrive(s + 1, *event)

            product(s, half, slot_of(half, p, q))

    finish(STAGES - 1)

    for s in range(STAGES):
        columns = pl.ds((s % CHUNKS) * COLS, COLS)
        out = out_one if s < CHUNKS else out_two
        for half in range(2):
            wait_all(g.at[s, half, pl.ds(0, PEERS - 1)], g_send.at[s, half])
        wait_all(up_recv.at[s, pl.ds(1, PEERS - 1)], up_ss.at[s])
        wait_all(par.at[s, pl.ds(1, rows - 1)], row_ss.at[s])
        wait_all(far_recv.at[s, pl.ds(1, PEERS - 1)], far_ss.at[s])
        pltpu.make_async_copy(t_buf.at[s], out.at[:, columns], out_sem.at[s]).wait()


def hand_on(one, two, out_one, out_two, held, sem):
    rows = LEAF // PARTS
    steps = []
    for i, (src, dst) in enumerate(((one, out_one), (two, out_two))):
        for j in range(PARTS):
            part = pl.ds(j * rows, rows)
            steps.append(
                (
                    pltpu.make_async_copy(src.at[part], held.at[i, part], sem.at[0, i, j]),
                    pltpu.make_async_copy(held.at[i, part], dst.at[part], sem.at[1, i, j]),
                )
            )
    for come, _ in steps:
        come.start()
    for come, go in steps:
        come.wait()
        go.start()
    for _, go in steps:
        go.wait()


def local(
    probes,
    near_blocks,
    near_leaves,
    near_count,
    leaf_rank,
    leaf_basis,
    leaf_transfer,
    leaf_links,
    leaf_link_blocks,
    parent_links,
    parent_link_blocks,
):
    rows = lax.axis_size("row")
    smem = pl.BlockSpec(memory_space=pltpu.SMEM)
    hbm = pl.BlockSpec(memory_space=pl.ANY)
    dma = pltpu.SemaphoreType.DMA
    vmem = pltpu.VMEM
    folded = (2 * SHARE, PARENT // 2)
    terms = pl.pallas_call(
        functools.partial(kernel, rows),
        out_shape=[jax.ShapeDtypeStruct((LEAF, PROBES), F32)] * 2,
        in_specs=[smem] * 5 + [hbm] * 6,
        out_specs=[hbm] * 2,
        scratch_shapes=[
            vmem((STAGES, 2, PEERS, BLOCK, COLS), BF),
            vmem((8, LEAF, LEAF), BF),
            vmem((LEAF, PROBES), F32),
            vmem((2, LEAF, COLS), F32),
            vmem((2, RANK, COLS), F32),
            vmem((STAGES, LEAF, COLS), F32),
            vmem((LEAF, RANK), F32),
            vmem((RANK, PARENT), F32),
            vmem((4, RANK, RANK), F32),
            vmem((2, PARENT, PARENT), F32),
            vmem((LEAF, RANK), BF),
            vmem((LEAF, RANK), BF),
            vmem((RANK, LEAF), BF),
            vmem((RANK, LEAF), BF),
            vmem((RANK, PARENT), BF),
            vmem((4, RANK, RANK), BF),
            vmem((2, PARENT, PARENT), BF),
            vmem((STAGES, PEERS, *folded), BF),
            vmem((STAGES, PEERS, *folded), BF),
            vmem((STAGES, rows, *folded), BF),
            vmem((STAGES, PEERS, *folded), BF),
            *[pltpu.SMEM((PEERS,), jnp.int32)] * 4,
            dma((6,)),
            dma((STAGES,)),
            dma((STAGES, 2)),
            dma((STAGES, 2, PEERS)),
            *[dma((STAGES,))] * 6,
        ],
        compiler_params=pltpu.CompilerParams(
            collective_id=0, has_side_effects=True, vmem_limit_bytes=62 * 2**20
        ),
    )(
        near_leaves, near_count, leaf_rank, leaf_links, parent_links,
        probes, near_blocks, leaf_basis, leaf_transfer, leaf_link_blocks, parent_link_blocks,
    )
    return pl.pallas_call(
        hand_on,
        out_shape=[jax.ShapeDtypeStruct((LEAF, PROBES), F32)] * 2,
        in_specs=[hbm] * 2,
        out_specs=[hbm] * 2,
        scratch_shapes=[vmem((2, LEAF, PROBES), F32), dma((2, 2, PARTS))],
    )(*terms)


def solution(mesh):
    in_specs = (
        P(("row", "col"), None),
        P(("row", "col"), None, None, None),
        P(("row", "col"), None),
        P(("row", "col")),
        P(("row", "col")),
        P(("row", "col"), None),
        P(("row", "col"), None, None),
        P(("row", "col"), None),
        P(("row", "col"), None, None, None),
        P("row", None),
        P("row", None, None, None),
    )
    out_specs = (P(("row", "col"), None), P(("row", "col"), None))
    return jax.shard_map(local, mesh=mesh, in_specs=in_specs, out_specs=out_specs, check_vma=False)
```
